512 devices in a mesh: slab: 32 (over z, core), row: 4 (over y), col: 4 (over x).
Axes of the slice: x: 4, y: 4, z: 16, core: 2. Of those that a mesh axis runs over, the one named last changes fastest.
Arguments:
- coupling: float32 [512, 512], replicated, may hold values from -1 to 1, as said below
- disorder: int32 [64, 512], P('slab'), may hold values from 0 to 1023
- gain_level: int32 [64, 512], P('slab'), may hold values from 0 to 3, as said below
Outputs:
- reduced: float32 [32, 2, 512, 512], P('slab', None, ('row', 'col'))
- coupled: float32 [32, 2, 512, 512], P('slab', None, ('row', 'col'))
The draws below stay inside these ranges and needn't reach their ends.
Inputs may be any that keep to these rules, and one draw needn't show every extreme that they name: symmetric: coupling[p, q] = coupling[q, p]. `gain_level`: in each slice the nonzero entries fill one run of 256 consecutive points and lie in 1 to 3; all other entries are 0.
All inputs are finite; a program needn't handle non-finite values.
Results may differ from the reference program's by a relative error of at most 0.00014.
Values sent between devices are 32-bit elements; how exact they have to be, the bound alone decides.
A program may use at most 64 MiB of HBM per device.

```python
import math
import jax
import jax.numpy as jnp
from jax import lax

POINTS = 512
DEGREE = 8
SLICES = 64


def draw_coupling(key, part):
    key = jax.random.fold_in(key, 11)
    entries = jax.random.truncated_normal(key, -4.0, 4.0, (POINTS, POINTS), jnp.float32)
    return (entries + entries.T) * (0.425 / math.sqrt(2.0 * POINTS))


def draw_gain_level(key, part):
    key = jax.random.fold_in(key, 23)
    start_key, level_key = jax.random.split(key)
    band_width = POINTS // 2
    starts = jax.random.randint(start_key, (SLICES, 1), 0, POINTS - band_width + 1)
    levels = jax.random.randint(level_key, (SLICES, POINTS), 1, 4)
    positions = jnp.arange(POINTS, dtype=jnp.int32)[None, :]
    inside = (positions >= starts) & (positions < starts + band_width)
    return jnp.where(inside, levels, 0).astype(jnp.int32)


def plant(array, stream_key, low, high):
    longest = array.shape.index(max(array.shape))
    spots = []
    for shift in (0, 1):
        where = [jax.random.randint(jax.random.fold_in(stream_key, axis), (), 0, length) for axis, length in enumerate(array.shape)]
        where[longest] = (where[longest] + shift) % array.shape[longest]
        spots.append(tuple(where))
    return array.at[spots[0]].set(low).at[spots[1]].set(high)


def setup_inputs(seed: int = 0) -> dict:
    arg_keys = jax.random.split(jax.random.key(seed), 4)
    return {
        "coupling": draw_coupling(jax.random.fold_in(arg_keys[3], 71), 0),
        "disorder": plant(jax.random.randint(arg_keys[1], (SLICES, POINTS), 0, 1024), jax.random.fold_in(arg_keys[1], 1), 0, 1023).astype(jnp.int32),
        "gain_level": draw_gain_level(jax.random.fold_in(arg_keys[3], 71), 0),
    }


energy_level = 0.5
absorption = 2.0
disorder_width = 2.0
gain_step = 0.25
hop_square = 2.25


def real_dot(first_factor, second_factor):
    return jnp.dot(first_factor, second_factor, precision=lax.Precision.HIGHEST, preferred_element_type=jnp.float32)


def complex_product(left_side, right_side):
    real_part = real_dot(left_side[0], right_side[0]) - real_dot(left_side[1], right_side[1])
    imag_part = real_dot(left_side[0], right_side[1]) + real_dot(left_side[1], right_side[0])
    return jnp.stack([real_part, imag_part])


def identity_rows(first_row, row_count, points):
    row_ids = jnp.arange(row_count, dtype=jnp.int32)[:, None] + first_row
    return (row_ids == jnp.arange(points, dtype=jnp.int32)[None, :]).astype(jnp.float32)


def slice_block(coupling_rows, potential_row, gain_row, identity):
    real_part = identity * (energy_level - potential_row)[None, :] - coupling_rows
    imag_part = identity * (absorption - gain_row)[None, :]
    return jnp.stack([real_part, imag_part])


def inverse_rows(matrix, first_row, row_count):
    points = matrix.shape[2]
    identity = identity_rows(0, points, points)
    diag_real = jnp.diagonal(matrix[0])
    diag_imag = jnp.diagonal(matrix[1])
    magnitude = diag_real * diag_real + diag_imag * diag_imag
    inv_real = diag_real / magnitude
    inv_imag = -diag_imag / magnitude
    residual = jnp.stack([identity - (matrix[0] * inv_real[None, :] - matrix[1] * inv_imag[None, :]),
                          -(matrix[0] * inv_imag[None, :] + matrix[1] * inv_real[None, :])])
    unit_real = identity_rows(first_row, row_count, points)
    unit_rows = jnp.stack([unit_real, jnp.zeros_like(unit_real)])
    series = lax.dynamic_slice_in_dim(residual, first_row, row_count, 1) + unit_rows
    for repeat in range(DEGREE - 1):
        series = unit_rows + complex_product(series, residual)
    scale_real = lax.dynamic_slice_in_dim(inv_real, first_row, row_count, 0)[:, None]
    scale_imag = lax.dynamic_slice_in_dim(inv_imag, first_row, row_count, 0)[:, None]
    return jnp.stack([scale_real * series[0] - scale_imag * series[1],
                      scale_real * series[1] + scale_imag * series[0]])


def reference(coupling, disorder, gain_level):
    points = coupling.shape[0]
    slab_total = disorder.shape[0] // 2
    identity = identity_rows(0, points, points)
    potential = disorder_width * (disorder.astype(jnp.float32) / 1023.0 - 0.5)
    gain_values = gain_step * gain_level.astype(jnp.float32)
    slab_numbers = jnp.arange(slab_total, dtype=jnp.int32)

    def odd_coupling(slab_number):
        matrix = slice_block(coupling, potential[2 * slab_number + 1], gain_values[2 * slab_number + 1], identity)
        return -hop_square * inverse_rows(matrix, 0, points)

    def even_block(slab_number):
        return slice_block(coupling, potential[2 * slab_number], gain_values[2 * slab_number], identity)

    couplings = lax.map(odd_coupling, slab_numbers)
    previous = jnp.concatenate([jnp.zeros_like(couplings[:1]), couplings[:-1]])
    even_blocks = lax.map(even_block, slab_numbers)
    first_reduction = even_blocks + couplings + previous

    def eliminate(slab_number):
        inverse = inverse_rows(first_reduction[slab_number], 0, points)
        before = previous[slab_number]
        ahead_term = couplings[slab_number]
        first_term = complex_product(before, inverse)
        second_term = complex_product(ahead_term, inverse)
        sent_blocks = complex_product(first_term, before)
        linked = -complex_product(first_term, ahead_term)
        forward = complex_product(second_term, ahead_term)
        return sent_blocks, linked, forward

    sent_blocks, linked, forward = lax.map(eliminate, slab_numbers)
    from_ahead = jnp.concatenate([sent_blocks[1:], jnp.zeros_like(sent_blocks[:1])])
    from_behind = jnp.concatenate([jnp.zeros_like(forward[:1]), forward[:-1]])
    reduced = first_reduction - from_ahead - from_behind
    coupled = jnp.concatenate([linked[1:], jnp.zeros_like(linked[:1])])
    return reduced, coupled
```

```python
import jax
import jax.numpy as jnp
from jax import lax
from jax.experimental import pallas as pl
from jax.experimental.pallas import tpu as pltpu
from jax.sharding import PartitionSpec as P

DEGREE = 8
MESH = pl.DeviceIdType.MESH
F32 = jnp.float32
BF16 = jnp.bfloat16

energy_level = 0.5
absorption = 2.0
disorder_width = 2.0
gain_step = 0.25
hop_square = 2.25

N = 512
B = 32
T = 128
RING = 4
CHUNK = 80


def dot(a, b):
    return jnp.dot(a, b, preferred_element_type=F32)


def split(a):
    hi = a.astype(BF16)
    return hi, (a - hi.astype(F32)).astype(BF16)


def product(hi, lo, both, weight_hi, weight_lo):
    rows = hi.shape[0]
    wide = dot(both, weight_hi)
    return (wide[:rows] + wide[rows:]) + dot(hi, weight_lo)


def kernel(coupling_hbm, disorder_ref, gain_ref, reduced_ref, coupled_ref,
           kf, kh, kl, a_buf, ab, acc, w, lband, chunks, lrh, lrl, lih, lil, fs_send, fs_recv,
           load_sem, a_send, a_recv, g_send, g_recv, f_send, f_recv):
    slab = lax.axis_index("slab")
    row = lax.axis_index("row")
    col = lax.axis_index("col")
    slabs = lax.axis_size("slab")
    band = (row * RING + col) * B
    ahead = lax.rem(slab + 1, slabs)
    behind = lax.rem(slab + slabs - 1, slabs)
    place = {"row": row, "col": col}

    def stepped(axis, step):
        return lax.rem(place[axis] + (step + RING), RING)

    load = pltpu.make_async_copy(coupling_hbm, kf, load_sem)
    load.start()

    barrier = pltpu.get_barrier_semaphore()
    for target in (ahead, behind):
        pl.semaphore_signal(barrier, inc=1, device_id={"slab": target}, device_id_type=MESH)
    for axis in ("row", "col"):
        for step in (1, -1):
            pl.semaphore_signal(barrier, inc=1, device_id={axis: stepped(axis, step)}, device_id_type=MESH)

    potential = disorder_width * (disorder_ref[...].astype(F32) / 1023.0 - 0.5)
    gain = gain_step * gain_ref[...].astype(F32)
    eye = lax.broadcasted_iota(jnp.int32, (T, T), 0) == lax.broadcasted_iota(jnp.int32, (T, T), 1)
    load.wait()
    k_diag = jnp.concatenate(
        [jnp.sum(jnp.where(eye, kf[t * T:(t + 1) * T, t * T:(t + 1) * T], 0.0), axis=0, keepdims=True)
         for t in range(N // T)], axis=1)
    d_re = (energy_level - potential[1:2]) - k_diag
    d_im = absorption - gain[1:2]
    size = d_re * d_re + d_im * d_im
    a_buf[1, 0:1, :] = d_re / size
    a_buf[1, 1:2, :] = -d_im / size

    pl.semaphore_wait(barrier, 6)
    a_copies = []
    for which, (target, slot) in enumerate(((ahead, 0), (behind, 2))):
        copy = pltpu.make_async_remote_copy(
            src_ref=a_buf.at[1], dst_ref=a_buf.at[slot], send_sem=a_send.at[which], recv_sem=a_recv.at[which],
            device_id={"slab": target}, device_id_type=MESH)
        copy.start()
        a_copies.append(copy)

    for t in range(N // T):
        rows = slice(t * T, (t + 1) * T)
        ids = lax.broadcasted_iota(jnp.int32, (T, N), 0) + t * T
        off = jnp.where(ids == lax.broadcasted_iota(jnp.int32, (T, N), 1), 0.0, kf[rows, :])
        hi, lo = split(off)
        kh[rows, :] = hi
        kl[rows, :] = lo

    def series(slots, count):
        def step(index, carry):
            hi, lo = split(acc[:2 * slots])
            t = product(hi, lo, jnp.concatenate([hi, lo], axis=0), kh[...], kl[...])
            t_re, t_im = t[:slots], t[slots:]
            a_re, a_im = ab[0, :slots], ab[1, :slots]
            acc[:slots] = w[:slots] + (t_re * a_re - t_im * a_im)
            acc[slots:2 * slots] = w[slots:2 * slots] + (t_re * a_im + t_im * a_re)
            return carry
        lax.fori_loop(0, count, step, 0)

    def spread(group, slot):
        for part in range(2):
            ab[part, group * B:(group + 1) * B, :] = jnp.broadcast_to(a_buf[slot, part:part + 1, :], (B, N))

    unit = (lax.broadcasted_iota(jnp.int32, (B, N), 0) + band) == lax.broadcasted_iota(jnp.int32, (B, N), 1)
    k_band = jnp.where(unit, 0.0, kf[pl.ds(pl.multiple_of(band, B), B), :])
    a_copies[0].wait_recv()
    spread(0, 0)
    spread(1, 1)
    for group in range(2):
        rows = slice(group * B, (group + 1) * B)
        rows_im = slice((2 + group) * B, (3 + group) * B)
        a_re, a_im = ab[0, rows, :], ab[1, rows, :]
        w_re = jnp.where(unit, -hop_square * a_re, 0.0)
        w_im = jnp.where(unit, -hop_square * a_im, 0.0)
        if group == 0:
            w_re = jnp.where(slab == 0, 0.0, w_re)
            w_im = jnp.where(slab == 0, 0.0, w_im)
        w[rows, :] = w_re
        w[rows_im, :] = w_im
        t_re = jnp.sum(w_re, axis=1, keepdims=True) * k_band
        t_im = jnp.sum(w_im, axis=1, keepdims=True) * k_band
        acc[rows, :] = w_re + (t_re * a_re - t_im * a_im)
        acc[rows_im, :] = w_im + (t_re * a_im + t_im * a_re)
    series(2 * B, DEGREE - 1)

    even_re = jnp.where(unit, energy_level - potential[0:1], 0.0) - kf[pl.ds(pl.multiple_of(band, B), B), :]
    even_im = jnp.where(unit, absorption - gain[0:1], 0.0)
    lband[0] = (even_re + acc[B:2 * B, :]) + acc[0:B, :]
    lband[1] = (even_im + acc[3 * B:4 * B, :]) + acc[2 * B:3 * B, :]
    tiles = []
    for distance in range(3):
        at = pl.ds(pl.multiple_of(lax.rem(row + distance, RING) * T, T), T)
        tiles.append((lband[0, :, at], lband[1, :, at]))
    far = jnp.where(row < 2, tiles[2][0], tiles[2][1])
    for part in range(2):
        chunks[part, row, col, 0:B, :] = tiles[0][part]
        chunks[part, row, col, B:2 * B, :] = tiles[1][part]
        chunks[part, row, col, 2 * B:CHUNK, :] = far[part * (B // 2):(part + 1) * (B // 2)]

    axes = (("col", "row"), ("row", "col"))
    HALF = CHUNK // 2
    pending = []

    def chunk(part, first, second, half=None):
        at = {axes[part][0]: stepped(axes[part][0], first), axes[part][1]: stepped(axes[part][1], second)}
        ref = chunks.at[part, at["row"], at["col"]]
        return ref if half is None else ref.at[pl.ds(half * HALF, HALF), :]

    def copy_of(ref, part, phase, stage, step):
        axis = axes[part][0 if stage == 0 else 1]
        number = stage * 4 + phase * 2 + (0 if step == 1 else 1)
        return pltpu.make_async_remote_copy(
            src_ref=ref, dst_ref=ref, send_sem=g_send.at[part, number], recv_sem=g_recv.at[part, number],
            device_id={axis: stepped(axis, step)}, device_id_type=MESH)

    def send(ref, part, phase, stage, step):
        copy = copy_of(ref, part, phase, stage, step)
        copy.start()
        pending.append(copy)

    def offset(stage, away, along):
        return (along, 0) if stage == 0 else (away, along)

    AWAY = (0, -1, 1, 2)

    def begin(part, stage):
        away = 0 if stage == 0 else AWAY[stage - 1]
        for step in (1, -1):
            send(chunk(part, *offset(stage, away, 0)), part, 0, stage, step)

    def forward(part, stage):
        away = 0 if stage == 0 else AWAY[stage - 1]
        for step in (1, -1):
            landed = offset(stage, away, -step)
            copy_of(chunk(part, *landed), part, 0, stage, step).wait_recv()
            send(chunk(part, *landed, 0 if step == 1 else 1), part, 1, stage, step)
            if stage == 0:
                begin(part, 2 if step == 1 else 3)

    def finish(part, stage):
        away = 0 if stage == 0 else AWAY[stage - 1]
        for step in (1, -1):
            copy_of(chunk(part, *offset(stage, away, 2), 0 if step == 1 else 1), part, 1, stage, step).wait_recv()

    for part in range(2):
        begin(part, 0)
        begin(part, 1)
    for part in range(2):
        forward(part, 0)
    for part in range(2):
        forward(part, 1)
    for part in range(2):
        finish(part, 0)
        begin(part, 4)
    for stage in (2, 3, 4):
        for part in range(2):
            forward(part, stage)
    for stage in (1, 2, 3, 4):
        for part in range(2):
            finish(part, stage)

    weights = ((lrh, lrl), (lih, lil))
    diagonal = [[], []]

    def put(part, r, c, tile):
        hi, lo = split(tile)
        weights[part][0][r * T:(r + 1) * T, c * T:(c + 1) * T] = hi
        weights[part][1][r * T:(r + 1) * T, c * T:(c + 1) * T] = lo

    for r in range(RING):
        for part in range(2):
            tile = chunks[part, r, :, 0:B, :].reshape(T, T)
            diagonal[part].append(jnp.sum(jnp.where(eye, tile, 0.0), axis=0, keepdims=True))
            put(part, r, r, jnp.where(eye, 0.0, tile))
            tile = chunks[part, r, :, B:2 * B, :].reshape(T, T)
            put(part, r, (r + 1) % RING, tile)
            put(part, (r + 1) % RING, r, tile.T)
        tile = jnp.concatenate([chunks[0, r, :, 2 * B:CHUNK, :], chunks[1, r, :, 2 * B:CHUNK, :]], axis=1).reshape(T, T)
        part = 0 if r < 2 else 1
        put(part, r, (r + 2) % RING, tile)
        put(part, (r + 2) % RING, r, tile.T)
    d_re = jnp.concatenate(diagonal[0], axis=1)
    d_im = jnp.concatenate(diagonal[1], axis=1)
    size = d_re * d_re + d_im * d_im
    i_re = d_re / size
    i_im = -d_im / size
    HB = 2 * B
    v_re, v_im = acc[:HB, :], acc[HB:2 * HB, :]
    w_re = v_re * i_re - v_im * i_im
    w_im = v_re * i_im + v_im * i_re
    w[:HB, :] = w_re
    w[HB:2 * HB, :] = w_im
    acc[:HB, :] = w_re
    acc[HB:2 * HB, :] = w_im

    def inverse_step(index, carry):
        hi, lo = split(acc[:2 * HB])
        both = jnp.concatenate([hi, lo], axis=0)
        t = product(hi, lo, both, lrh[...], lrl[...])
        u = product(hi, lo, both, lih[...], lil[...])
        t_re = t[:HB] - u[HB:]
        t_im = t[HB:] + u[:HB]
        acc[:HB, :] = w[:HB, :] - (t_re * i_re - t_im * i_im)
        acc[HB:2 * HB, :] = w[HB:2 * HB, :] - (t_re * i_im + t_im * i_re)
        return carry
    lax.fori_loop(0, DEGREE, inverse_step, 0)

    f_copies = []
    for which, target in enumerate((behind, ahead)):
        for part in range(2):
            fs_send[which, part] = acc[part * HB + which * B:part * HB + (which + 1) * B, :]
        copy = pltpu.make_async_remote_copy(
            src_ref=fs_send.at[which], dst_ref=fs_recv.at[which], send_sem=f_send.at[which], recv_sem=f_recv.at[which],
            device_id={"slab": target}, device_id_type=MESH)
        copy.start()
        f_copies.append(copy)

    a_copies[1].wait_recv()
    for group, slot in enumerate((1, 2, 0)):
        spread(group, slot)
    GB = 3 * B
    for group, which in enumerate((0, 0, 1)):
        if group != 1:
            f_copies[which].wait_recv()
        rows = slice(group * B, (group + 1) * B)
        rows_im = slice(GB + group * B, GB + (group + 1) * B)
        a_re, a_im = ab[0, rows, :], ab[1, rows, :]
        v_re = -hop_square * fs_recv[which, 0]
        v_im = -hop_square * fs_recv[which, 1]
        w_re = v_re * a_re - v_im * a_im
        w_im = v_re * a_im + v_im * a_re
        w[rows, :] = w_re
        w[rows_im, :] = w_im
        acc[rows, :] = w_re
        acc[rows_im, :] = w_im
    series(GB, DEGREE)
    first, last = slab == 0, slab == slabs - 1
    for part in range(2):
        base = part * GB
        x = jnp.where(last, 0.0, acc[base:base + B, :])
        z = jnp.where(last, 0.0, -acc[base + B:base + 2 * B, :])
        y = jnp.where(first, 0.0, acc[base + 2 * B:base + 3 * B, :])
        reduced_ref[part] = (lband[part] - x) - y
        coupled_ref[part] = z

    for copy in a_copies + pending + f_copies:
        copy.wait_send()


def local(coupling, disorder, gain_level):
    vmem = pl.BlockSpec(memory_space=pltpu.VMEM)
    scratch = [
        pltpu.VMEM((N, N), F32),
        pltpu.VMEM((N, N), BF16),
        pltpu.VMEM((N, N), BF16),
        pltpu.VMEM((3, 8, N), F32),
        pltpu.VMEM((2, 3 * B, N), F32),
        pltpu.VMEM((6 * B, N), F32),
        pltpu.VMEM((6 * B, N), F32),
        pltpu.VMEM((2, B, N), F32),
        pltpu.VMEM((2, RING, RING, CHUNK, T), F32),
        pltpu.VMEM((N, N), BF16),
        pltpu.VMEM((N, N), BF16),
        pltpu.VMEM((N, N), BF16),
        pltpu.VMEM((N, N), BF16),
        pltpu.VMEM((2, 2, B, N), F32),
        pltpu.VMEM((2, 2, B, N), F32),
        pltpu.SemaphoreType.DMA,
        pltpu.SemaphoreType.DMA((2,)),
        pltpu.SemaphoreType.DMA((2,)),
        pltpu.SemaphoreType.DMA((2, 20)),
        pltpu.SemaphoreType.DMA((2, 20)),
        pltpu.SemaphoreType.DMA((2,)),
        pltpu.SemaphoreType.DMA((2,)),
    ]
    reduced, coupled = pl.pallas_call(
        kernel,
        out_shape=[jax.ShapeDtypeStruct((2, B, N), F32)] * 2,
        in_specs=[pl.BlockSpec(memory_space=pl.ANY), vmem, vmem],
        out_specs=[vmem, vmem],
        scratch_shapes=scratch,
        compiler_params=pltpu.CompilerParams(
            collective_id=0, has_side_effects=True, vmem_limit_bytes=32 * 2**20),
        cost_estimate=pl.CostEstimate(flops=8 * 10**9, bytes_accessed=2 * 2**20, transcendentals=0),
        name="reduce_two_levels",
    )(coupling, disorder, gain_level)
    return reduced[None], coupled[None]


def solution(mesh):
    return jax.shard_map(
        local,
        mesh=mesh,
        in_specs=(P(), P("slab", None), P("slab", None)),
        out_specs=(P("slab", None, ("row", "col"), None), P("slab", None, ("row", "col"), None)),
        check_vma=False,
    )
```

```python
import jax
import jax.numpy as jnp
from jax import lax
from jax.experimental import pallas as pl
from jax.experimental.pallas import tpu as pltpu
from jax.sharding import PartitionSpec as P

DEGREE = 8
MESH = pl.DeviceIdType.MESH
F32 = jnp.float32
BF16 = jnp.bfloat16

energy_level = 0.5
absorption = 2.0
disorder_width = 2.0
gain_step = 0.25
hop_square = 2.25

N = 512
B = 32
T = 128
H = 256
LOW, HIGH, ALL = slice(0, H), slice(H, N), slice(0, N)


def dot(a, b):
    return jnp.dot(a, b, preferred_element_type=F32)


def split(a):
    hi = a.astype(BF16)
    return hi, (a - hi.astype(F32)).astype(BF16)


def product(hi, lo, weight_hi, weight_lo):
    return (dot(hi, weight_hi) + dot(lo, weight_hi)) + dot(hi, weight_lo)


def times(a_re, a_im, b_re, b_im):
    return a_re * b_re - a_im * b_im, a_re * b_im + a_im * b_re


def kernel(coupling_hbm, disorder_hbm, gain_hbm, reduced_ref, coupled_ref,
           kf, kh, kl, levels, a_buf, a_cols, w, q, qh, ql, m, mh, ml, lh, ll,
           acc, base, lband, x_send, z_send, y_send, x_recv, z_recv, y_recv,
           load_sem, a_sems, x_sems, z_sems, y_sems):
    slab = lax.axis_index("slab")
    band = (lax.axis_index("row") * lax.axis_size("col") + lax.axis_index("col")) * B
    slabs = lax.axis_size("slab")
    has_behind, has_ahead = slab > 0, slab < slabs - 1
    ahead, behind = jnp.minimum(slab + 1, slabs - 1), jnp.maximum(slab - 1, 0)

    loads = [pltpu.make_async_copy(source, target, load_sem.at[number]) for number, (source, target) in enumerate(
        ((disorder_hbm, levels.at[0]), (gain_hbm, levels.at[1]), (coupling_hbm, kf)))]
    for load in loads:
        load.start()

    barrier = pltpu.get_barrier_semaphore()

    @pl.when(has_ahead)
    def _():
        pl.semaphore_signal(barrier, inc=1, device_id={"slab": ahead}, device_id_type=MESH)

    @pl.when(has_behind)
    def _():
        pl.semaphore_signal(barrier, inc=1, device_id={"slab": behind}, device_id_type=MESH)

    def remote(source, target, sems, device):
        return pltpu.make_async_remote_copy(
            src_ref=source, dst_ref=target, send_sem=sems.at[0], recv_sem=sems.at[1],
            device_id={"slab": device}, device_id_type=MESH)

    a_copy = remote(a_buf.at[1], a_buf.at[0], a_sems, ahead)
    x_copy = remote(x_send, x_recv, x_sems, behind)
    z_copy = remote(z_send, z_recv, z_sems, behind)
    y_copy = remote(y_send, y_recv, y_sems, ahead)

    eye = lax.broadcasted_iota(jnp.int32, (T, T), 0) == lax.broadcasted_iota(jnp.int32, (T, T), 1)

    def diagonal_of(ref):
        return jnp.concatenate(
            [jnp.sum(jnp.where(eye, ref[t * T:(t + 1) * T, t * T:(t + 1) * T], 0.0), axis=0, keepdims=True)
             for t in range(N // T)], axis=1)

    loads[0].wait()
    loads[1].wait()
    potential = disorder_width * (levels[0].astype(F32) / 1023.0 - 0.5)
    gain = gain_step * levels[1].astype(F32)
    loads[2].wait()
    k_diag = diagonal_of(kf)
    d_re = (energy_level - potential) - k_diag
    d_im = absorption - gain
    size = d_re[1:2] * d_re[1:2] + d_im[1:2] * d_im[1:2]
    a_buf[1, 0:1, :] = d_re[1:2] / size
    a_buf[1, 1:2, :] = -d_im[1:2] / size

    for t in range(N // T):
        rows = slice(t * T, (t + 1) * T)
        ids = lax.broadcasted_iota(jnp.int32, (T, N), 0) + t * T
        off = jnp.where(ids == lax.broadcasted_iota(jnp.int32, (T, N), 1), 0.0, kf[rows, :])
        kf[rows, :] = off
        hi, lo = split(off)
        kh[rows, :] = hi
        kl[rows, :] = lo

    def mirror(ref, part):
        ref[part, LOW, HIGH] = ref[part, HIGH, LOW].T

    def whole_m(which, a_re, a_im, after_first):
        for t in range(N // T):
            cols = slice(t * T, (t + 1) * T)
            a_cols[0, cols, :] = jnp.broadcast_to(a_re[:, cols], (T, T)).T
            a_cols[1, cols, :] = jnp.broadcast_to(a_im[:, cols], (T, T)).T

        def scaled(rows):
            re, im = times(w[0, rows, :], w[1, rows, :], a_re, a_im)
            return split(jnp.concatenate([re, im], axis=0))

        for step in range(3):
            for rows, cols in ((LOW, LOW), (HIGH, ALL)):
                if step == 0:
                    hi, lo = split(jnp.concatenate([kf[rows, :] * a_re, kf[rows, :] * a_im], axis=0))
                else:
                    hi, lo = scaled(rows)
                t = product(hi, lo, kh[:, cols], kl[:, cols])
                w[0, rows, cols] = t[:H]
                w[1, rows, cols] = t[H:]
                if step == 0:
                    q[0, rows, cols] = kf[rows, cols] + t[:H]
                    q[1, rows, cols] = t[H:]
                elif step == 1:
                    q[0, rows, cols] = q[0, rows, cols] + t[:H]
                    q[1, rows, cols] = q[1, rows, cols] + t[H:]
                else:
                    q[0, rows, cols] = q[0, rows, cols] + t[:H]
                    q[1, rows, cols] = q[1, rows, cols] + t[H:]
            for part in range(2):
                mirror(w, part)
            if step == 0:
                after_first()
        for part in range(2):
            mirror(q, part)
            hi, lo = split(q[part])
            qh[part] = hi
            ql[part] = lo
        for rows, cols in ((LOW, LOW), (HIGH, ALL)):
            hi, lo = scaled(rows)
            t = product(hi, lo, qh[0, :, cols], ql[0, :, cols])
            u = product(hi, lo, qh[1, :, cols], ql[1, :, cols])
            n_re = q[0, rows, cols] + (t[:H] - u[H:])
            n_im = q[1, rows, cols] + (t[H:] + u[:H])
            n_re, n_im = times(n_re, n_im, a_re[:, cols], a_im[:, cols])
            width = n_re.shape[1]
            diagonal = ((lax.broadcasted_iota(jnp.int32, (H, width), 0) + rows.start)
                        == (lax.broadcasted_iota(jnp.int32, (H, width), 1) + cols.start))
            n_re = n_re + jnp.where(diagonal, 1.0, 0.0)
            c_re = jnp.concatenate([a_cols[0, rows, :]] * (width // T), axis=1) * -hop_square
            c_im = jnp.concatenate([a_cols[1, rows, :]] * (width // T), axis=1) * -hop_square
            m_re, m_im = times(n_re, n_im, c_re, c_im)
            m[which, 0, rows, cols] = m_re
            m[which, 1, rows, cols] = m_im
        for part in range(2):
            mirror(m.at[which], part)
            hi, lo = split(m[which, part])
            mh[which, part] = hi
            ml[which, part] = lo

    def meet():
        pl.semaphore_wait(barrier, has_ahead.astype(jnp.int32) + has_behind.astype(jnp.int32))

        @pl.when(has_ahead)
        def _():
            a_copy.start()

    whole_m(1, a_buf[1, 0:1, :], a_buf[1, 1:2, :], meet)

    @pl.when(has_behind)
    def _():
        a_copy.wait_recv()

    whole_m(0, jnp.where(has_behind, a_buf[0, 0:1, :], 0.0), jnp.where(has_behind, a_buf[0, 1:2, :], 0.0), lambda: None)

    m_diag = [[diagonal_of(m.at[which, part]) for part in range(2)] for which in range(2)]
    d_re = (d_re[0:1] + m_diag[1][0]) + m_diag[0][0]
    d_im = (d_im[0:1] + m_diag[1][1]) + m_diag[0][1]
    size = d_re * d_re + d_im * d_im
    i_re = d_re / size
    i_im = -d_im / size
    for t in range(N // T):
        rows = slice(t * T, (t + 1) * T)
        off = (lax.broadcasted_iota(jnp.int32, (T, N), 0) + t * T) != lax.broadcasted_iota(jnp.int32, (T, N), 1)
        hi, lo = split(jnp.where(off, (m[1, 0, rows, :] - kf[rows, :]) + m[0, 0, rows, :], 0.0))
        lh[0, rows, :] = hi
        ll[0, rows, :] = lo
        hi, lo = split(jnp.where(off, m[1, 1, rows, :] + m[0, 1, rows, :], 0.0))
        lh[1, rows, :] = hi
        ll[1, rows, :] = lo
    mine = pl.ds(pl.multiple_of(band, B), B)
    unit = (lax.broadcasted_iota(jnp.int32, (B, N), 0) + band) == lax.broadcasted_iota(jnp.int32, (B, N), 1)
    lband[0] = jnp.where(unit, d_re, (m[1, 0, mine, :] - kf[mine, :]) + m[0, 0, mine, :])
    lband[1] = jnp.where(unit, d_im, m[1, 1, mine, :] + m[0, 1, mine, :])

    W2 = 2 * B
    for which in range(2):
        re, im = times(m[which, 0, mine, :], m[which, 1, mine, :], i_re, i_im)
        for ref in (base, acc):
            ref[which * B:(which + 1) * B, :] = re
            ref[W2 + which * B:W2 + (which + 1) * B, :] = im

    def by_complex(rows, hi_ref, lo_ref):
        hi, lo = split(rows)
        half = rows.shape[0] // 2
        both = jnp.concatenate([hi, lo], axis=0)
        t = dot(both, hi_ref[0])
        t = (t[:2 * half] + t[2 * half:]) + dot(hi, lo_ref[0])
        u = dot(both, hi_ref[1])
        u = (u[:2 * half] + u[2 * half:]) + dot(hi, lo_ref[1])
        return t[:half] - u[half:], t[half:] + u[:half]

    def inverse_step(index, carry):
        re, im = times(*by_complex(acc[...], lh, ll), i_re, i_im)
        acc[:W2, :] = base[:W2, :] - re
        acc[W2:, :] = base[W2:, :] - im
        return carry
    lax.fori_loop(0, DEGREE, inverse_step, 0)

    terms = by_complex(acc[...], mh.at[1], ml.at[1])
    for part in range(2):
        z_send[part] = -terms[part][:B]
        y_send[part] = terms[part][B:]

    @pl.when(has_behind)
    def _():
        z_copy.start()

    @pl.when(has_ahead)
    def _():
        y_copy.start()
    first = jnp.concatenate([acc[0:B, :], acc[W2:W2 + B, :]], axis=0)
    terms = by_complex(first, mh.at[0], ml.at[0])
    for part in range(2):
        x_send[part] = terms[part]

    @pl.when(has_behind)
    def _():
        x_copy.start()
        y_copy.wait_recv()

    @pl.when(has_ahead)
    def _():
        z_copy.wait_recv()
        x_copy.wait_recv()
    reduced_ref[...] = (lband[...] - jnp.where(has_ahead, x_recv[...], 0.0)) - jnp.where(has_behind, y_recv[...], 0.0)
    coupled_ref[...] = jnp.where(has_ahead, z_recv[...], 0.0)

    @pl.when(has_behind)
    def _():
        z_copy.wait_send()
        x_copy.wait_send()

    @pl.when(has_ahead)
    def _():
        a_copy.wait_send()
        y_copy.wait_send()


def local(coupling, disorder, gain_level):
    vmem = pl.BlockSpec(memory_space=pltpu.VMEM)
    hbm = pl.BlockSpec(memory_space=pl.ANY)
    square = (N, N)
    band = pltpu.VMEM((2, B, N), F32)
    pair = pltpu.SemaphoreType.DMA((2,))
    scratch = [
        pltpu.VMEM(square, F32),
        pltpu.VMEM(square, BF16),
        pltpu.VMEM(square, BF16),
        pltpu.VMEM((2, 2, N), jnp.int32),
        pltpu.VMEM((2, 8, N), F32),
        pltpu.VMEM((2, N, T), F32),
        pltpu.VMEM((2,) + square, F32),
        pltpu.VMEM((2,) + square, F32),
        pltpu.VMEM((2,) + square, BF16),
        pltpu.VMEM((2,) + square, BF16),
        pltpu.VMEM((2, 2) + square, F32),
        pltpu.VMEM((2, 2) + square, BF16),
        pltpu.VMEM((2, 2) + square, BF16),
        pltpu.VMEM((2,) + square, BF16),
        pltpu.VMEM((2,) + square, BF16),
        pltpu.VMEM((4 * B, N), F32),
        pltpu.VMEM((4 * B, N), F32),
        band, band, band, band, band, band, band,
        pltpu.SemaphoreType.DMA((3,)),
        pair, pair, pair, pair,
    ]
    reduced, coupled = pl.pallas_call(
        kernel,
        out_shape=[jax.ShapeDtypeStruct((2, B, N), F32)] * 2,
        in_specs=[hbm, hbm, hbm],
        out_specs=[vmem, vmem],
        scratch_shapes=scratch,
        compiler_params=pltpu.CompilerParams(
            collective_id=0, has_side_effects=True, vmem_limit_bytes=32 * 2**20),
        cost_estimate=pl.CostEstimate(flops=16 * 10**9, bytes_accessed=2 * 2**20, transcendentals=0),
        name="reduce_two_levels",
    )(coupling, disorder, gain_level)
    return reduced[None], coupled[None]


def solution(mesh):
    return jax.shard_map(
        local,
        mesh=mesh,
        in_specs=(P(), P("slab", None), P("slab", None)),
        out_specs=(P("slab", None, ("row", "col"), None), P("slab", None, ("row", "col"), None)),
        check_vma=False,
    )
```

```python
import jax
import jax.numpy as jnp
from jax import lax
from jax.experimental import pallas as pl
from jax.experimental.pallas import tpu as pltpu
from jax.sharding import PartitionSpec as P

DEGREE = 8
MESH = pl.DeviceIdType.MESH
F32 = jnp.float32
BF16 = jnp.bfloat16

energy_level = 0.5
absorption = 2.0
disorder_width = 2.0
gain_step = 0.25
hop_square = 2.25

N = 512
B = 32
T = 128
H = 256
LOW, HIGH, ALL = slice(0, H), slice(H, N), slice(0, N)


def dot(a, b):
    return jnp.dot(a, b, preferred_element_type=F32)


def split(a):
    hi = a.astype(BF16)
    return hi, (a - hi.astype(F32)).astype(BF16)


def product(hi, lo, weight_hi, weight_lo):
    return (dot(hi, weight_hi) + dot(lo, weight_hi)) + dot(hi, weight_lo)


def times(a_re, a_im, b_re, b_im):
    return a_re * b_re - a_im * b_im, a_re * b_im + a_im * b_re


def kernel(coupling_ref, potential_ref, gain_ref, kept_ref, y_ref, minus_z_ref,
           kf, kh, kl, a_buf, a_cols, w, q, qh, ql, m, mh, ml, lh, ll,
           acc, base, lband, f_send, z_send, s_send, f_recv, z_recv, s_recv,
           a_sems, f_sems, z_sems, s_sems):
    slab = lax.axis_index("slab")
    band = (lax.axis_index("row") * lax.axis_size("col") + lax.axis_index("col")) * B
    slabs = lax.axis_size("slab")
    has_behind, has_ahead = slab > 0, slab < slabs - 1
    ahead, behind = jnp.minimum(slab + 1, slabs - 1), jnp.maximum(slab - 1, 0)

    barrier = pltpu.get_barrier_semaphore()

    @pl.when(has_ahead)
    def _():
        pl.semaphore_signal(barrier, inc=1, device_id={"slab": ahead}, device_id_type=MESH)

    @pl.when(has_behind)
    def _():
        pl.semaphore_signal(barrier, inc=1, device_id={"slab": behind}, device_id_type=MESH)

    def remote(source, target, sems, device):
        return pltpu.make_async_remote_copy(
            src_ref=source, dst_ref=target, send_sem=sems.at[0], recv_sem=sems.at[1],
            device_id={"slab": device}, device_id_type=MESH)

    a_copy = remote(a_buf.at[1], a_buf.at[0], a_sems, ahead)
    f_copy = remote(f_send, f_recv, f_sems, behind)
    z_copy = remote(z_send, z_recv, z_sems, behind)
    s_copy = remote(s_send, s_recv, s_sems, ahead)

    eye = lax.broadcasted_iota(jnp.int32, (T, T), 0) == lax.broadcasted_iota(jnp.int32, (T, T), 1)

    def diagonal_of(ref):
        return jnp.concatenate(
            [jnp.sum(jnp.where(eye, ref[t * T:(t + 1) * T, t * T:(t + 1) * T], 0.0), axis=0, keepdims=True)
             for t in range(N // T)], axis=1)

    potential = potential_ref[...]
    gain = gain_ref[...]
    k_diag = diagonal_of(coupling_ref)
    d_re = (energy_level - potential) - k_diag
    d_im = absorption - gain
    size = d_re[1:2] * d_re[1:2] + d_im[1:2] * d_im[1:2]
    a_buf[1, 0:1, :] = d_re[1:2] / size
    a_buf[1, 1:2, :] = -d_im[1:2] / size

    for t in range(N // T):
        rows = slice(t * T, (t + 1) * T)
        ids = lax.broadcasted_iota(jnp.int32, (T, N), 0) + t * T
        off = jnp.where(ids == lax.broadcasted_iota(jnp.int32, (T, N), 1), 0.0, coupling_ref[rows, :])
        kf[rows, :] = off
        hi, lo = split(off)
        kh[rows, :] = hi
        kl[rows, :] = lo

    def whole_m(which, a_re, a_im, after_first):
        for t in range(N // T):
            cols = slice(t * T, (t + 1) * T)
            a_cols[0, cols, :] = jnp.broadcast_to(a_re[:, cols], (T, T)).T
            a_cols[1, cols, :] = jnp.broadcast_to(a_im[:, cols], (T, T)).T

        blocks = [(slice(r, r + T), ALL if r >= H else LOW) for r in (2 * T, 3 * T, 0, T)]

        def scaled(step, rows):
            if step == 0:
                re, im = kf[rows, :] * a_re, kf[rows, :] * a_im
            else:
                re, im = times(w[step - 1, 0, rows, :], w[step - 1, 1, rows, :], a_re, a_im)
            return re, im

        def mirror(ref, rows):
            if rows.start >= H:
                for part in range(2):
                    ref[part, LOW, rows] = ref[part, rows, LOW].T

        for step in range(3):
            for rows, cols in blocks:
                hi, lo = split(jnp.concatenate(scaled(step, rows), axis=0))
                t = product(hi, lo, kh[:, cols], kl[:, cols])
                w[step, 0, rows, cols] = t[:T]
                w[step, 1, rows, cols] = t[T:]
                mirror(w.at[step], rows)
            if step == 0:
                after_first()
        for part in range(2):
            for rows in (HIGH, LOW):
                total = (w[0, part, rows, :] + w[1, part, rows, :]) + w[2, part, rows, :]
                if part == 0:
                    total = total + kf[rows, :]
                q[part, rows, :] = total
                hi, lo = split(total)
                qh[part, rows, :] = hi
                ql[part, rows, :] = lo
        for rows in (HIGH, LOW):
            hi, lo = split(q[0, rows, :] + q[1, rows, :])
            qh[2, rows, :] = hi
            ql[2, rows, :] = lo
        for rows, cols in blocks:
            re, im = scaled(3, rows)
            both_re = product(*split(re), qh[0, :, cols], ql[0, :, cols])
            both_im = product(*split(im), qh[1, :, cols], ql[1, :, cols])
            crossed = product(*split(re + im), qh[2, :, cols], ql[2, :, cols])
            n_re = q[0, rows, cols] + (both_re - both_im)
            n_im = q[1, rows, cols] + ((crossed - both_re) - both_im)
            n_re, n_im = times(n_re, n_im, a_re[:, cols], a_im[:, cols])
            width = n_re.shape[1]
            diagonal = ((lax.broadcasted_iota(jnp.int32, (T, width), 0) + rows.start)
                        == (lax.broadcasted_iota(jnp.int32, (T, width), 1) + cols.start))
            n_re = n_re + jnp.where(diagonal, 1.0, 0.0)
            c_re = jnp.concatenate([a_cols[0, rows, :]] * (width // T), axis=1) * -hop_square
            c_im = jnp.concatenate([a_cols[1, rows, :]] * (width // T), axis=1) * -hop_square
            m_re, m_im = times(n_re, n_im, c_re, c_im)
            m[which, 0, rows, cols] = m_re
            m[which, 1, rows, cols] = m_im
            mirror(m.at[which], rows)
        for part in range(2):
            hi, lo = split(m[which, part])
            mh[which, part] = hi
            ml[which, part] = lo

    def meet():
        pl.semaphore_wait(barrier, has_ahead.astype(jnp.int32) + has_behind.astype(jnp.int32))

        @pl.when(has_ahead)
        def _():
            a_copy.start()

    whole_m(1, a_buf[1, 0:1, :], a_buf[1, 1:2, :], meet)

    @pl.when(has_behind)
    def _():
        a_copy.wait_recv()

    whole_m(0, jnp.where(has_behind, a_buf[0, 0:1, :], 0.0), jnp.where(has_behind, a_buf[0, 1:2, :], 0.0), lambda: None)

    m_diag = [[diagonal_of(m.at[which, part]) for part in range(2)] for which in range(2)]
    d_re = (d_re[0:1] + m_diag[1][0]) + m_diag[0][0]
    d_im = (d_im[0:1] + m_diag[1][1]) + m_diag[0][1]
    size = d_re * d_re + d_im * d_im
    i_re = d_re / size
    i_im = -d_im / size
    for t in range(N // T):
        rows = slice(t * T, (t + 1) * T)
        off = (lax.broadcasted_iota(jnp.int32, (T, N), 0) + t * T) != lax.broadcasted_iota(jnp.int32, (T, N), 1)
        hi, lo = split(jnp.where(off, (m[1, 0, rows, :] - kf[rows, :]) + m[0, 0, rows, :], 0.0))
        lh[0, rows, :] = hi
        ll[0, rows, :] = lo
        hi, lo = split(jnp.where(off, m[1, 1, rows, :] + m[0, 1, rows, :], 0.0))
        lh[1, rows, :] = hi
        ll[1, rows, :] = lo
    mine = pl.ds(pl.multiple_of(band, B), B)
    unit = (lax.broadcasted_iota(jnp.int32, (B, N), 0) + band) == lax.broadcasted_iota(jnp.int32, (B, N), 1)
    lband[0] = jnp.where(unit, d_re, (m[1, 0, mine, :] - kf[mine, :]) + m[0, 0, mine, :])
    lband[1] = jnp.where(unit, d_im, m[1, 1, mine, :] + m[0, 1, mine, :])

    W2 = 2 * B
    for which in range(2):
        re, im = times(m[which, 0, mine, :], m[which, 1, mine, :], i_re, i_im)
        for ref in (base, acc):
            ref[which * B:(which + 1) * B, :] = re
            ref[W2 + which * B:W2 + (which + 1) * B, :] = im

    def by_complex(rows, hi_ref, lo_ref):
        hi, lo = split(rows)
        half = rows.shape[0] // 2
        both = jnp.concatenate([hi, lo], axis=0)
        t = dot(both, hi_ref[0])
        t = (t[:2 * half] + t[2 * half:]) + dot(hi, lo_ref[0])
        u = dot(both, hi_ref[1])
        u = (u[:2 * half] + u[2 * half:]) + dot(hi, lo_ref[1])
        return t[:half] - u[half:], t[half:] + u[:half]

    def inverse_step(index, carry):
        re, im = times(*by_complex(acc[...], lh, ll), i_re, i_im)
        acc[:W2, :] = base[:W2, :] - re
        acc[W2:, :] = base[W2:, :] - im
        return carry
    lax.fori_loop(0, DEGREE, inverse_step, 0)

    for part in range(2):
        f_send[part * B:(part + 1) * B, :] = acc[part * W2:part * W2 + B, :]
        s_send[part * B:(part + 1) * B, :] = acc[part * W2 + B:(part + 1) * W2, :]

    @pl.when(has_behind)
    def _():
        f_copy.start()

    @pl.when(has_ahead)
    def _():
        s_copy.start()
    terms = by_complex(f_send[...], mh.at[1], ml.at[1])
    for part in range(2):
        z_send[part] = terms[part]

    @pl.when(has_behind)
    def _():
        z_copy.start()
        s_copy.wait_recv()
    terms = by_complex(jnp.where(has_behind, s_recv[...], 0.0), mh.at[0], ml.at[0])
    for part in range(2):
        y_ref[part] = terms[part]

    @pl.when(has_ahead)
    def _():
        f_copy.wait_recv()
    terms = by_complex(jnp.where(has_ahead, f_recv[...], 0.0), mh.at[1], ml.at[1])
    for part in range(2):
        kept_ref[part] = lband[part] - terms[part]

    @pl.when(has_ahead)
    def _():
        z_copy.wait_recv()
    minus_z_ref[...] = jnp.where(has_ahead, z_recv[...], 0.0)

    @pl.when(has_behind)
    def _():
        f_copy.wait_send()
        z_copy.wait_send()

    @pl.when(has_ahead)
    def _():
        a_copy.wait_send()
        s_copy.wait_send()


def local(coupling, disorder, gain_level):
    vmem = pl.BlockSpec(memory_space=pltpu.VMEM)
    square = (N, N)
    band = pltpu.VMEM((2, B, N), F32)
    rows = pltpu.VMEM((2 * B, N), F32)
    potential = disorder_width * (disorder.astype(F32) / 1023.0 - 0.5)
    gain = gain_step * gain_level.astype(F32)
    pair = pltpu.SemaphoreType.DMA((2,))
    scratch = [
        pltpu.VMEM(square, F32),
        pltpu.VMEM(square, BF16),
        pltpu.VMEM(square, BF16),
        pltpu.VMEM((2, 8, N), F32),
        pltpu.VMEM((2, N, T), F32),
        pltpu.VMEM((3, 2) + square, F32),
        pltpu.VMEM((2,) + square, F32),
        pltpu.VMEM((3,) + square, BF16),
        pltpu.VMEM((3,) + square, BF16),
        pltpu.VMEM((2, 2) + square, F32),
        pltpu.VMEM((2, 2) + square, BF16),
        pltpu.VMEM((2, 2) + square, BF16),
        pltpu.VMEM((2,) + square, BF16),
        pltpu.VMEM((2,) + square, BF16),
        pltpu.VMEM((4 * B, N), F32),
        pltpu.VMEM((4 * B, N), F32),
        band, rows, band, rows, rows, band, rows,
        pair, pair, pair, pair,
    ]
    kept, y, minus_z = pl.pallas_call(
        kernel,
        out_shape=[jax.ShapeDtypeStruct((2, B, N), F32)] * 3,
        in_specs=[vmem, vmem, vmem],
        out_specs=[vmem, vmem, vmem],
        scratch_shapes=scratch,
        compiler_params=pltpu.CompilerParams(
            collective_id=0, has_side_effects=True, vmem_limit_bytes=32 * 2**20),
        cost_estimate=pl.CostEstimate(flops=16 * 10**9, bytes_accessed=2 * 2**20, transcendentals=0),
        name="reduce_two_levels",
    )(coupling, potential, gain)
    return (kept - y)[None], (-minus_z)[None]


def solution(mesh):
    return jax.shard_map(
        local,
        mesh=mesh,
        in_specs=(P(), P("slab", None), P("slab", None)),
        out_specs=(P("slab", None, ("row", "col"), None), P("slab", None, ("row", "col"), None)),
        check_vma=False,
    )
```

```python
import jax
import jax.numpy as jnp
from jax import lax
from jax.experimental import pallas as pl
from jax.experimental.pallas import tpu as pltpu
from jax.sharding import PartitionSpec as P

DEGREE = 8
MESH = pl.DeviceIdType.MESH
F32 = jnp.float32
BF16 = jnp.bfloat16

energy_level = 0.5
absorption = 2.0
disorder_width = 2.0
gain_step = 0.25
hop_square = 2.25

N = 512
B = 32
T = 128
H = 256
LOW, HIGH, ALL = slice(0, H), slice(H, N), slice(0, N)


def dot(a, b):
    return jnp.dot(a, b, preferred_element_type=F32)


def split(a):
    hi = a.astype(BF16)
    return hi, (a - hi.astype(F32)).astype(BF16)


def product(hi, lo, weight_hi, weight_lo):
    return (dot(hi, weight_hi) + dot(lo, weight_hi)) + dot(hi, weight_lo)


def times(a_re, a_im, b_re, b_im):
    return a_re * b_re - a_im * b_im, a_re * b_im + a_im * b_re


def kernel(minus_k_ref, disorder_ref, gain_ref, kept_ref, y_ref, minus_z_ref,
           kf, kh, kl, a_buf, a_cols, w, q, qh, ql, m, mh, ml, lh, ll,
           acc, base, lband, f_send, z_send, s_send, f_recv, z_recv, s_recv,
           a_sems, f_sems, z_sems, s_sems):
    slab = lax.axis_index("slab")
    band = (lax.axis_index("row") * lax.axis_size("col") + lax.axis_index("col")) * B
    slabs = lax.axis_size("slab")
    has_behind, has_ahead = slab > 0, slab < slabs - 1
    ahead, behind = jnp.minimum(slab + 1, slabs - 1), jnp.maximum(slab - 1, 0)

    barrier = pltpu.get_barrier_semaphore()

    @pl.when(has_ahead)
    def _():
        pl.semaphore_signal(barrier, inc=1, device_id={"slab": ahead}, device_id_type=MESH)

    @pl.when(has_behind)
    def _():
        pl.semaphore_signal(barrier, inc=1, device_id={"slab": behind}, device_id_type=MESH)

    def remote(source, target, sems, device):
        return pltpu.make_async_remote_copy(
            src_ref=source, dst_ref=target, send_sem=sems.at[0], recv_sem=sems.at[1],
            device_id={"slab": device}, device_id_type=MESH)

    a_copy = remote(a_buf.at[1], a_buf.at[0], a_sems, ahead)
    f_copy = remote(f_send, f_recv, f_sems, behind)
    z_copy = remote(z_send, z_recv, z_sems, behind)
    s_copy = remote(s_send, s_recv, s_sems, ahead)

    eye = lax.broadcasted_iota(jnp.int32, (T, T), 0) == lax.broadcasted_iota(jnp.int32, (T, T), 1)

    def diagonal_of(ref):
        return jnp.concatenate(
            [jnp.sum(jnp.where(eye, ref[t * T:(t + 1) * T, t * T:(t + 1) * T], 0.0), axis=0, keepdims=True)
             for t in range(N // T)], axis=1)

    potential = disorder_width * (disorder_ref[...].astype(F32) / 1023.0 - 0.5)
    gain = gain_step * gain_ref[...].astype(F32)
    d_re = (energy_level - potential) + diagonal_of(minus_k_ref)
    d_im = absorption - gain
    size = d_re[1:2] * d_re[1:2] + d_im[1:2] * d_im[1:2]
    a_buf[1, 0:1, :] = d_re[1:2] / size
    a_buf[1, 1:2, :] = -d_im[1:2] / size

    for t in range(N // T):
        rows = slice(t * T, (t + 1) * T)
        ids = lax.broadcasted_iota(jnp.int32, (T, N), 0) + t * T
        off = jnp.where(ids == lax.broadcasted_iota(jnp.int32, (T, N), 1), 0.0, -minus_k_ref[rows, :])
        kf[rows, :] = off
        hi, lo = split(off)
        kh[rows, :] = hi
        kl[rows, :] = lo

    def whole_m(which, a_re, a_im, after_first):
        for t in range(N // T):
            cols = slice(t * T, (t + 1) * T)
            a_cols[0, cols, :] = jnp.broadcast_to(a_re[:, cols], (T, T)).T
            a_cols[1, cols, :] = jnp.broadcast_to(a_im[:, cols], (T, T)).T

        blocks = [(slice(r, r + T), ALL if r >= H else LOW) for r in (2 * T, 3 * T, 0, T)]

        def scaled(step, rows):
            if step == 0:
                re, im = kf[rows, :] * a_re, kf[rows, :] * a_im
            else:
                re, im = times(w[step - 1, 0, rows, :], w[step - 1, 1, rows, :], a_re, a_im)
            return re, im

        def mirror(ref, rows):
            if rows.start >= H:
                for part in range(2):
                    ref[part, LOW, rows] = ref[part, rows, LOW].T

        for step in range(3):
            for rows, cols in blocks:
                hi, lo = split(jnp.concatenate(scaled(step, rows), axis=0))
                t = product(hi, lo, kh[:, cols], kl[:, cols])
                w[step, 0, rows, cols] = t[:T]
                w[step, 1, rows, cols] = t[T:]
                mirror(w.at[step], rows)
            if step == 0:
                after_first()
        for part in range(2):
            for rows in (HIGH, LOW):
                total = (w[0, part, rows, :] + w[1, part, rows, :]) + w[2, part, rows, :]
                if part == 0:
                    total = total + kf[rows, :]
                q[part, rows, :] = total
                hi, lo = split(total)
                qh[part, rows, :] = hi
                ql[part, rows, :] = lo
        for rows in (HIGH, LOW):
            hi, lo = split(q[0, rows, :] + q[1, rows, :])
            qh[2, rows, :] = hi
            ql[2, rows, :] = lo
        for rows, cols in blocks:
            re, im = scaled(3, rows)
            both_re = product(*split(re), qh[0, :, cols], ql[0, :, cols])
            both_im = product(*split(im), qh[1, :, cols], ql[1, :, cols])
            crossed = product(*split(re + im), qh[2, :, cols], ql[2, :, cols])
            n_re = q[0, rows, cols] + (both_re - both_im)
            n_im = q[1, rows, cols] + ((crossed - both_re) - both_im)
            n_re, n_im = times(n_re, n_im, a_re[:, cols], a_im[:, cols])
            width = n_re.shape[1]
            diagonal = ((lax.broadcasted_iota(jnp.int32, (T, width), 0) + rows.start)
                        == (lax.broadcasted_iota(jnp.int32, (T, width), 1) + cols.start))
            n_re = n_re + jnp.where(diagonal, 1.0, 0.0)
            c_re = jnp.concatenate([a_cols[0, rows, :]] * (width // T), axis=1) * -hop_square
            c_im = jnp.concatenate([a_cols[1, rows, :]] * (width // T), axis=1) * -hop_square
            m_re, m_im = times(n_re, n_im, c_re, c_im)
            m[which, 0, rows, cols] = m_re
            m[which, 1, rows, cols] = m_im
            mirror(m.at[which], rows)
        for part in range(2):
            hi, lo = split(m[which, part])
            mh[which, part] = hi
            ml[which, part] = lo

    def meet():
        pl.semaphore_wait(barrier, has_ahead.astype(jnp.int32) + has_behind.astype(jnp.int32))

        @pl.when(has_ahead)
        def _():
            a_copy.start()

    whole_m(1, a_buf[1, 0:1, :], a_buf[1, 1:2, :], meet)

    @pl.when(has_behind)
    def _():
        a_copy.wait_recv()

    whole_m(0, jnp.where(has_behind, a_buf[0, 0:1, :], 0.0), jnp.where(has_behind, a_buf[0, 1:2, :], 0.0), lambda: None)

    m_diag = [[diagonal_of(m.at[which, part]) for part in range(2)] for which in range(2)]
    d_re = (d_re[0:1] + m_diag[1][0]) + m_diag[0][0]
    d_im = (d_im[0:1] + m_diag[1][1]) + m_diag[0][1]
    size = d_re * d_re + d_im * d_im
    i_re = d_re / size
    i_im = -d_im / size
    for t in range(N // T):
        rows = slice(t * T, (t + 1) * T)
        off = (lax.broadcasted_iota(jnp.int32, (T, N), 0) + t * T) != lax.broadcasted_iota(jnp.int32, (T, N), 1)
        hi, lo = split(jnp.where(off, (m[1, 0, rows, :] - kf[rows, :]) + m[0, 0, rows, :], 0.0))
        lh[0, rows, :] = hi
        ll[0, rows, :] = lo
        hi, lo = split(jnp.where(off, m[1, 1, rows, :] + m[0, 1, rows, :], 0.0))
        lh[1, rows, :] = hi
        ll[1, rows, :] = lo
    mine = pl.ds(pl.multiple_of(band, B), B)
    unit = (lax.broadcasted_iota(jnp.int32, (B, N), 0) + band) == lax.broadcasted_iota(jnp.int32, (B, N), 1)
    lband[0] = jnp.where(unit, d_re, (m[1, 0, mine, :] - kf[mine, :]) + m[0, 0, mine, :])
    lband[1] = jnp.where(unit, d_im, m[1, 1, mine, :] + m[0, 1, mine, :])

    W2 = 2 * B
    for which in range(2):
        re, im = times(m[which, 0, mine, :], m[which, 1, mine, :], i_re, i_im)
        for ref in (base, acc):
            ref[which * B:(which + 1) * B, :] = re
            ref[W2 + which * B:W2 + (which + 1) * B, :] = im

    def by_complex(rows, hi_ref, lo_ref):
        hi, lo = split(rows)
        half = rows.shape[0] // 2
        both = jnp.concatenate([hi, lo], axis=0)
        t = dot(both, hi_ref[0])
        t = (t[:2 * half] + t[2 * half:]) + dot(hi, lo_ref[0])
        u = dot(both, hi_ref[1])
        u = (u[:2 * half] + u[2 * half:]) + dot(hi, lo_ref[1])
        return t[:half] - u[half:], t[half:] + u[:half]

    def inverse_steps(index, carry):
        rows = acc[...]
        for repeat in range(2):
            re, im = times(*by_complex(rows, lh, ll), i_re, i_im)
            rows = base[...] - jnp.concatenate([re, im], axis=0)
        acc[...] = rows
        return carry
    lax.fori_loop(0, DEGREE // 2, inverse_steps, 0)

    for part in range(2):
        f_send[part * B:(part + 1) * B, :] = acc[part * W2:part * W2 + B, :]
        s_send[part * B:(part + 1) * B, :] = acc[part * W2 + B:(part + 1) * W2, :]

    @pl.when(has_behind)
    def _():
        f_copy.start()

    @pl.when(has_ahead)
    def _():
        s_copy.start()
    terms = by_complex(f_send[...], mh.at[1], ml.at[1])
    for part in range(2):
        z_send[part] = terms[part]

    @pl.when(has_behind)
    def _():
        z_copy.start()
        s_copy.wait_recv()
    terms = by_complex(jnp.where(has_behind, s_recv[...], 0.0), mh.at[0], ml.at[0])
    for part in range(2):
        y_ref[part] = terms[part]

    @pl.when(has_ahead)
    def _():
        f_copy.wait_recv()
    terms = by_complex(jnp.where(has_ahead, f_recv[...], 0.0), mh.at[1], ml.at[1])
    for part in range(2):
        kept_ref[part] = lband[part] - terms[part]

    @pl.when(has_ahead)
    def _():
        z_copy.wait_recv()
    minus_z_ref[...] = jnp.where(has_ahead, z_recv[...], 0.0)

    @pl.when(has_behind)
    def _():
        f_copy.wait_send()
        z_copy.wait_send()

    @pl.when(has_ahead)
    def _():
        a_copy.wait_send()
        s_copy.wait_send()


def local(coupling, disorder, gain_level):
    vmem = pl.BlockSpec(memory_space=pltpu.VMEM)
    square = (N, N)
    band = pltpu.VMEM((2, B, N), F32)
    rows = pltpu.VMEM((2 * B, N), F32)
    minus_k, disorder, gain_level = (-coupling, disorder, gain_level)
    pair = pltpu.SemaphoreType.DMA((2,))
    scratch = [
        pltpu.VMEM(square, F32),
        pltpu.VMEM(square, BF16),
        pltpu.VMEM(square, BF16),
        pltpu.VMEM((2, 8, N), F32),
        pltpu.VMEM((2, N, T), F32),
        pltpu.VMEM((3, 2) + square, F32),
        pltpu.VMEM((2,) + square, F32),
        pltpu.VMEM((3,) + square, BF16),
        pltpu.VMEM((3,) + square, BF16),
        pltpu.VMEM((2, 2) + square, F32),
        pltpu.VMEM((2, 2) + square, BF16),
        pltpu.VMEM((2, 2) + square, BF16),
        pltpu.VMEM((2,) + square, BF16),
        pltpu.VMEM((2,) + square, BF16),
        pltpu.VMEM((4 * B, N), F32),
        pltpu.VMEM((4 * B, N), F32),
        band, rows, band, rows, rows, band, rows,
        pair, pair, pair, pair,
    ]
    kept, y, minus_z = pl.pallas_call(
        kernel,
        out_shape=[jax.ShapeDtypeStruct((2, B, N), F32)] * 3,
        in_specs=[vmem, vmem, vmem],
        out_specs=[vmem, vmem, vmem],
        scratch_shapes=scratch,
        compiler_params=pltpu.CompilerParams(
            collective_id=0, has_side_effects=True, vmem_limit_bytes=32 * 2**20),
        cost_estimate=pl.CostEstimate(flops=16 * 10**9, bytes_accessed=2 * 2**20, transcendentals=0),
        name="reduce_two_levels",
    )(minus_k, disorder, gain_level)
    return (kept - y)[None], (-minus_z)[None]


def solution(mesh):
    return jax.shard_map(
        local,
        mesh=mesh,
        in_specs=(P(), P("slab", None), P("slab", None)),
        out_specs=(P("slab", None, ("row", "col"), None), P("slab", None, ("row", "col"), None)),
        check_vma=False,
    )
```
